256 devices in a mesh: outer: 16 (over z, y_lo), inner: 16 (over y_hi, x, core).
Axes of the slice: x: 4, y: 4 (y_hi: 2, y_lo: 2; y = y_hi * 2 + y_lo), z: 8, core: 2. Of those that a mesh axis runs over, the one named last changes fastest.
Arguments:
- tokens: bfloat16 [65536, 8192], P(('outer', 'inner')), may hold values from -6 to 6
- norm_gain: float32 [8192], replicated, may hold values from 0.25 to 1.75
- weight_codes: bfloat16 [8192, 512], P('inner'), may hold values from -1 to 1
- weight_scales: float32 [64, 512], P('inner'), may hold values from 0.006 to 0.04
- key_grad: bfloat16 [65536, 512], P(('outer', 'inner')), may hold values from -24 to 24
Outputs:
- key_out: bfloat16 [65536, 512], P(('outer', 'inner'))
- token_grad: bfloat16 [65536, 8192], P(('outer', 'inner'))
- weight_grad: float32 [8192, 512], P('inner', 'outer')
The draws below stay inside these ranges and needn't reach their ends.
All inputs are finite; a program needn't handle non-finite values. Where the reference program divides by a largest or mean magnitude, that divisor is 1e-20 or more.
Results may differ from the reference program's by a relative error of at most 0.015.
Values may be sent and summed in bfloat16 or wider, within the bound.
No kernel may reach another device: no remote copies, remote signals or barrier semaphores. Data moves between devices by JAX's collectives and lax.ppermute only.
A program may use at most 192 MiB of HBM per device.

```python
import math
import jax
import jax.numpy as jnp
from jax import lax

D = 8192
GROUP = 128
TOK_DEV = 256
KW = 512
TOKENS = 65536
N_OUTER = 16
N_INNER = 16


def strengthened(result, stream_key, source, target, blocks, factor):
    owner, partner = [(jnp.arange(result.shape[position]) // (result.shape[position] // blocks)).reshape([-1 if axis == position else 1 for axis in range(result.ndim)]) for position in (source, target)]
    chosen = jax.random.permutation(stream_key, blocks)[partner]
    strong = (owner == chosen) | (owner == (partner + blocks // 2) % blocks)
    return jnp.where(strong, factor * result, result)


def steps_of(rng, extent, cuts, least, largest):
    level = 1.0
    for dim, shards_of in cuts:
        heights = jax.random.uniform(jax.random.fold_in(jax.random.fold_in(rng, 6), dim), (shards_of,), jnp.float32, least / len(cuts), largest / len(cuts))
        level = level * jnp.repeat(jnp.exp(heights), extent[dim] // shards_of).reshape((-1,) + (1,) * (len(extent) - 1 - dim))
    return level


def noise(rng, shape, scale, most, pieces=(), kind=jnp.bfloat16):
    array = scale * jax.random.normal(rng, shape, jnp.float32)
    if pieces:
        array = array * steps_of(rng, shape, pieces, -0.22, 0.18)
    return jnp.clip(array, -most, most).astype(kind)


def gaussian_with(key, extent, width, most, shards, heavy, kind=jnp.bfloat16):
    array = width * jax.random.normal(key, extent, jnp.float32)
    if shards:
        array = array * steps_of(key, extent, shards, -0.22, 0.18)
    return jnp.clip(strengthened(array, jax.random.fold_in(key, 3), *heavy), -most, most).astype(kind)


def setup_inputs(seed: int = 0) -> dict:
    key_list = jax.random.split(jax.random.key(seed), 6)
    tokens = noise(key_list[0], (TOKENS, D), 1.0, 6.0, ((0, 256),))
    norm_gain = jnp.clip(1.0 + 0.15 * jax.random.normal(key_list[1], (D,), jnp.float32), 0.25, 1.75)
    weight_codes = jnp.clip(jax.random.uniform(key_list[2], (D, KW), jnp.float32, -1.0, 1.0) * steps_of(key_list[2], (D, KW), ((0, 16),), -0.4, 0.0), -1.0, 1.0).astype(jnp.bfloat16)
    weight_scales = jnp.clip(jnp.exp(math.log(0.04) - 1.89712 * jax.random.uniform(key_list[3], (D // GROUP, KW), jnp.float32) ** steps_of(key_list[3], (D // GROUP, KW), ((0, 16),), -0.2, 0.2)), 0.006, 0.04)
    key_grad = gaussian_with(key_list[4], (TOKENS, KW), 1.0, 24.0, ((0, 256),), (0, 1, 256, 6.0))
    return {"tokens": tokens, "norm_gain": norm_gain, "weight_codes": weight_codes, "weight_scales": weight_scales, "key_grad": key_grad}


def quantize(matrix):
    shape = matrix.shape
    groups = matrix.reshape(shape[:-2] + (shape[-2] // GROUP, GROUP, shape[-1]))
    group_scale = lax.optimization_barrier(jnp.max(jnp.abs(groups), axis=-2)) + 1e-06
    code_vals = (groups / group_scale[..., None, :]).astype(jnp.bfloat16)
    return (code_vals, group_scale)

def restore(code_vals, group_scale):
    values = code_vals.astype(jnp.float32) * group_scale[..., None, :]
    return values.reshape(code_vals.shape[:-3] + (-1, code_vals.shape[-1]))

def reference(tokens, norm_gain, weight_codes, weight_scales, key_grad):
    values = tokens.astype(jnp.float32)
    mean_square = lax.optimization_barrier(jnp.mean(values * values, axis=-1, keepdims=True))
    inverse = lax.rsqrt(mean_square + 1e-05)
    normed = (values * inverse * norm_gain).astype(jnp.bfloat16)
    weight = (weight_codes.reshape(D // GROUP, GROUP, KW).astype(jnp.float32) * weight_scales[:, None, :]).astype(jnp.bfloat16).reshape(D, KW)
    key_out = jnp.dot(normed, weight, preferred_element_type=jnp.float32).astype(jnp.bfloat16)
    back_grad = lax.dot_general(key_grad, weight, (((1,), (1,)), ((), ())), preferred_element_type=jnp.float32)
    scaled = back_grad * norm_gain
    average = lax.optimization_barrier(jnp.mean(values * scaled, axis=-1, keepdims=True))
    token_grad = (inverse * scaled - values * inverse ** 3 * average).astype(jnp.bfloat16)
    blocks_x = normed.reshape(N_OUTER, N_INNER, TOK_DEV, D)
    blocks_k = key_grad.reshape(N_OUTER, N_INNER, TOK_DEV, KW)

    def advance(running, blocks):
        block_x, block_k = blocks
        partial_value = jnp.einsum('itd,itk->idk', block_x.astype(jnp.float32), block_k.astype(jnp.float32))
        code_vals, group_scale = quantize(partial_value)
        summed = lax.optimization_barrier(jnp.sum(restore(code_vals, group_scale), axis=0))
        second_codes, second_scale = quantize(summed)
        return (running + restore(second_codes, second_scale), None)
    weight_grad, _ = lax.scan(advance, jnp.zeros((D, KW), jnp.float32), (blocks_x, blocks_k))
    return (key_out, token_grad, weight_grad)
```

```python
import functools

import jax
import jax.numpy as jnp
import numpy as np
from jax import lax
from jax.experimental import pallas as pl
from jax.experimental.pallas import tpu as pltpu
from jax.sharding import Mesh, PartitionSpec as P

BF, F32 = jnp.bfloat16, jnp.float32
NZ, NYL, NYH, NX, NC = 8, 2, 2, 4, 2
BLK, HALF = 512, 256
ROWS = (((0,), (0,)), ((), ()))
COLS = (((1,), (1,)), ((), ()))


def around(axis, size, step):
    return functools.partial(
        lax.ppermute, axis_name=axis, perm=[(i, (i + step) % size) for i in range(size)]
    )


def y_rank(y):
    return (y % 2) * 2 + (y // 2) % 2


def along_y(step):
    return functools.partial(
        lax.ppermute,
        axis_name=("yl", "yh"),
        perm=[(y_rank(y), y_rank((y + step) % 4)) for y in range(4)],
    )


swap_core = around("c", NC, 1)
swap_yh = around("yh", NYH, 1)


def vmem():
    return pl.BlockSpec(memory_space=pltpu.VMEM)


def smem():
    return pl.BlockSpec(memory_space=pltpu.SMEM)


def partial_kernel(where, tok_own, tok_far, kgt, *outs):
    x, yl, yh, c = where[0], where[1], where[2], where[3]

    def product(row0, rows, block, offset):
        own_col = pl.multiple_of((block * NC + c) * BLK + offset, HALF)
        far_col = pl.multiple_of(block * BLK + offset, HALF)
        left = kgt[pl.ds(row0, rows), :]
        return jnp.dot(
            left[:, :256], tok_own[:, pl.ds(own_col, HALF)], preferred_element_type=F32
        ) + jnp.dot(left[:, 256:], tok_far[:, pl.ds(far_col, HALF)], preferred_element_type=F32)

    for step in range(4):
        to = (x + step) % NX
        for h in range(NYH):
            outs[step][:, h * HALF : (h + 1) * HALF] = product(0, 512, h * NX + to, 0).astype(BF)
    y = yh * 2 + yl
    for step in range(4):
        to = (y + step) % 4
        row0 = pl.multiple_of((to % 2) * 256, 256)
        for q in range(NX):
            outs[4 + step][:, q * HALF : (q + 1) * HALF] = product(
                row0, 256, (to // 2) * NX + q, HALF
            ).astype(BF)


def partials(where, tok_own, tok_far, kgt):
    shapes = [jax.ShapeDtypeStruct((512, 512), BF)] * 4 + [
        jax.ShapeDtypeStruct((256, 1024), BF)
    ] * 4
    return pl.pallas_call(
        partial_kernel,
        out_shape=shapes,
        in_specs=[smem()] + [vmem()] * 3,
        out_specs=[vmem()] * 8,
        compiler_params=pltpu.CompilerParams(vmem_limit_bytes=40 * 2**20),
        cost_estimate=pl.CostEstimate(
            flops=2 * 512 * 512 * 4096, bytes_accessed=11 * 2**20, transcendentals=0
        ),
    )(where, tok_own, tok_far, kgt)


def project_kernel(where, tok_own, tok_far, kg, *refs):
    pieces, (key_own, key_far, grad_own, grad_far) = refs[:-4], refs[-4:]
    x, yh, c = where[0], where[2], where[3]
    key_own[...] = jnp.zeros_like(key_own)
    key_far[...] = jnp.zeros_like(key_far)
    for index in range(16):
        kind, hop, flip = index // 8, (index // 2) % 4, index % 2
        block = (yh + flip) % NYH * NX + (x + NX - hop) % NX
        offset = kind * HALF
        own_col = pl.multiple_of((block * NC + c) * BLK + offset, HALF)
        far_col = pl.multiple_of(block * BLK + offset, HALF)
        if kind == 0:
            weight = pieces[flip][hop * HALF : (hop + 1) * HALF, :]
        else:
            weight = pieces[2 + hop][flip * HALF : (flip + 1) * HALF, :]
        key_own[...] += jnp.dot(
            tok_own[:, pl.ds(own_col, HALF)], weight, preferred_element_type=F32
        )
        key_far[...] += jnp.dot(
            tok_far[:, pl.ds(far_col, HALF)], weight, preferred_element_type=F32
        )
        grads = lax.dot_general(kg[...], weight, COLS, preferred_element_type=F32).astype(BF)
        grad_own[:, pl.ds(far_col, HALF)] = grads[:256]
        grad_far[:, pl.ds(far_col, HALF)] = grads[256:]


def project(where, tok_own, tok_far, kg, pieces):
    return pl.pallas_call(
        project_kernel,
        out_shape=[jax.ShapeDtypeStruct((256, 512), F32)] * 2
        + [jax.ShapeDtypeStruct((256, 4096), BF)] * 2,
        in_specs=[smem()] + [vmem()] * (3 + len(pieces)),
        out_specs=[vmem()] * 4,
        compiler_params=pltpu.CompilerParams(vmem_limit_bytes=40 * 2**20),
        cost_estimate=pl.CostEstimate(
            flops=4 * 512 * 512 * 4096, bytes_accessed=16 * 2**20, transcendentals=0
        ),
    )(where, tok_own, tok_far, kg, *pieces)


def finish_kernel(where, tokens, grad_a, grad_b, slope, out):
    c = where[3]
    for block in range(NYH * NX):
        for refs, parity in ((grad_a, c), (grad_b, 1 - c)):
            col = pl.multiple_of((block * NC + parity) * BLK, BLK)
            part = refs[:, block * BLK : (block + 1) * BLK].astype(F32)
            values = tokens[:, pl.ds(col, BLK)].astype(F32)
            out[:, pl.ds(col, BLK)] = (part - values * slope[...]).astype(BF)


def finish(where, tokens, grad_a, grad_b, slope):
    return pl.pallas_call(
        finish_kernel,
        out_shape=jax.ShapeDtypeStruct((256, 8192), BF),
        in_specs=[smem()] + [vmem()] * 4,
        out_specs=vmem(),
        compiler_params=pltpu.CompilerParams(vmem_limit_bytes=40 * 2**20),
        cost_estimate=pl.CostEstimate(
            flops=2 * 256 * 8192, bytes_accessed=12 * 2**20, transcendentals=0
        ),
    )(where, tokens, grad_a, grad_b, slope)


def total(parts):
    out = parts[0].astype(F32)
    for part in parts[1:]:
        out = out + part.astype(F32)
    return out


def on_device(tokens, norm_gain, weight_codes, weight_scales, key_grad):
    x, yl, yh, c, z = [lax.axis_index(name) for name in ("x", "yl", "yh", "c", "z")]
    where = jnp.stack([x, yl, yh, c]).astype(jnp.int32)
    y = yh * 2 + yl
    shard = (yh * NX + x) * NC + c

    gain = lax.dynamic_slice(norm_gain, (shard * BLK,), (BLK,))
    weight = (
        weight_codes.reshape(4, 128, 512).astype(F32)
        * weight_scales[:, None, :]
        * gain.reshape(4, 128, 1)
    ).astype(BF).reshape(BLK, 512)
    w_a, w_b = weight[:HALF], weight[HALF:]
    a_parts = [w_a] + [around("x", NX, s)(w_a) for s in (1, 2, 3)]
    b_pair = jnp.concatenate([w_b, swap_yh(w_b)], axis=0)
    a_row = jnp.concatenate(a_parts, axis=0)
    pieces = [a_row, swap_yh(a_row), b_pair] + [around("x", NX, s)(b_pair) for s in (1, 2, 3)]

    blocks = tokens.reshape(256, NYH * NX, NC, BLK)
    send = lax.dynamic_index_in_dim(blocks, 1 - c, axis=2, keepdims=False).reshape(256, 4096)
    tok_far = swap_core(send)
    values = tokens.astype(F32)
    inverse = lax.rsqrt(jnp.mean(values * values, axis=-1, keepdims=True) + 1e-05)
    kg = (key_grad.astype(F32) * inverse).astype(BF)
    kg_both = jnp.concatenate([kg, swap_core(kg)], axis=0)
    kgt = (
        kg_both.T.reshape(NZ, NYL, 32, 512).transpose(1, 0, 2, 3).reshape(512, 512)
    )

    outs = partials(where, tokens, tok_far, kgt)
    a_sum = total([outs[0]] + [around("x", NX, s)(outs[s]) for s in (1, 2, 3)])
    b_sum = total([outs[4]] + [along_y(s)(outs[4 + s]) for s in (1, 2, 3)])
    a_sum = a_sum.astype(BF).reshape(NYL, 256, NYH, HALF)
    b_sum = b_sum.astype(BF).reshape(256, NX, HALF)

    def a_piece(step):
        to = (y + step) % 4
        return lax.dynamic_slice(a_sum, (to % 2, 0, to // 2, 0), (1, 256, 1, HALF)).reshape(256, HALF)

    def b_piece(step):
        to = (x + step) % NX
        return lax.dynamic_slice(b_sum, (0, to, 0), (256, 1, HALF)).reshape(256, HALF)

    a_done = total([a_piece(0)] + [along_y(s)(a_piece(s)) for s in (1, 2, 3)])
    b_done = total([b_piece(0)] + [around("x", NX, s)(b_piece(s)) for s in (1, 2, 3)])
    plane = jnp.concatenate([a_done, b_done], axis=1).astype(BF).reshape(NZ, 32, BLK)
    over_z = lax.all_to_all(plane, "z", split_axis=0, concat_axis=0, tiled=True)
    weight_grad = (jnp.sum(over_z.astype(F32), axis=0) * gain[None, :]).T

    key_own, key_far, grad_own, grad_far = project(where, tokens, tok_far, kg_both, pieces)
    key_sum = key_own + swap_core(key_far)
    key_out = (key_sum * inverse).astype(BF)
    dotted = jnp.sum(key_grad.astype(F32) * key_sum, axis=-1, keepdims=True) / 8192.0
    slope = inverse * inverse * inverse * dotted
    token_grad = finish(where, tokens, grad_own, swap_core(grad_far), slope)
    return key_out, token_grad, weight_grad


def solution(mesh):
    fine = Mesh(
        np.asarray(mesh.devices).reshape(NZ, NYL, NYH, NX, NC), ("z", "yl", "yh", "x", "c")
    )
    outer, inner = ("z", "yl"), ("yh", "x", "c")
    in_specs = (P(outer + inner, None), P(), P(inner, None), P(inner, None), P(outer + inner, None))
    out_specs = (P(outer + inner, None), P(outer + inner, None), P(inner, outer))
    return jax.shard_map(
        on_device, mesh=fine, in_specs=in_specs, out_specs=out_specs, check_vma=False
    )
```

```python
import jax
import jax.numpy as jnp
import numpy as np
from jax import lax
from jax.experimental import pallas as pl
from jax.experimental.pallas import tpu as pltpu
from jax.sharding import Mesh, PartitionSpec as P

BF, F32 = jnp.bfloat16, jnp.float32
NZ, NYL, NYH, NX, NC = 8, 2, 2, 4, 2
AXES = ("z", "yl", "yh", "x", "c")
SIZES = (NZ, NYL, NYH, NX, NC)
BLK, HALF = 512, 256
COLS = (((1,), (1,)), ((), ()))


def permute(array, target):
    pairs = []
    for flat_id in range(256):
        z, yl, yh, x, c = np.unravel_index(flat_id, SIZES)
        to = target(z, yh * 2 + yl, x, c)
        if to is not None:
            z, y, x, c = to[0] % NZ, to[1] % 4, to[2] % NX, to[3] % NC
            pairs.append((flat_id, int(np.ravel_multi_index((z, y % 2, y // 2, x, c), SIZES))))
    return lax.ppermute(array, AXES, pairs)


def swap_core(array):
    return permute(array, lambda z, y, x, c: (z, y, x, c + 1))


def first_axis(array, step):
    return permute(
        array, lambda z, y, x, c: (z, y, x + step, c) if c == 0 else (z, y + step, x, c)
    )


def second_axis(array, step):
    return permute(
        array, lambda z, y, x, c: (z, y + step, x, c) if c == 0 else (z, y, x + step, c)
    )


def gather_first(array, step):
    def target(z, y, x, c):
        if c == 0:
            return z, y, x + step, c
        return (z, y + 2, x, c) if step == 1 else None

    return permute(array, target)


def gather_second(array, step):
    def target(z, y, x, c):
        if c == 1:
            return z, y, x + step, c
        return (z, y + 2, x, c) if step < 3 else None

    return permute(array, target)


def along_z(array, step):
    return permute(array, lambda z, y, x, c: (z + step, y, x, c))


def vmem():
    return pl.BlockSpec(memory_space=pltpu.VMEM)


def smem():
    return pl.BlockSpec(memory_space=pltpu.SMEM)


def anywhere():
    return pl.BlockSpec(memory_space=pl.ANY)


def call(kernel, name, outs, grid_args, limit, flops, size, **kw):
    return pl.pallas_call(
        kernel,
        name=name,
        out_shape=outs,
        compiler_params=pltpu.CompilerParams(vmem_limit_bytes=limit * 2**20),
        cost_estimate=pl.CostEstimate(flops=flops, bytes_accessed=size, transcendentals=0),
        **grid_args,
        **kw,
    )


def arr(shape, dtype=BF):
    return jax.ShapeDtypeStruct(shape, dtype)


def flat(inputs, outputs, unused=0):
    return dict(
        in_specs=[smem()] + [vmem()] * inputs + [anywhere()] * unused,
        out_specs=[vmem()] * outputs,
    )


def rows_spec(cols):
    return pl.BlockSpec((32, cols), lambda r: (r, 0))


def weight_kernel(where, codes, scales, gain, out):
    half = where[4] % 2
    column = jnp.broadcast_to(gain[pl.ds(where[5], 1), :], (8, BLK)).T[:, :1]
    for group in range(2):
        rows = pl.ds(pl.multiple_of(half * HALF + group * 128, 128), 128)
        values = codes[rows, :].astype(F32) * scales[pl.ds(half * 2 + group, 1), :]
        part = jnp.where(
            half == 0, column[group * 128 : group * 128 + 128], column[HALF + group * 128 :][:128]
        )
        out[group * 128 : group * 128 + 128, :] = (values * part).astype(BF)


def prep_kernel(where, tokens, key_grad, after, send, scaled, inverse):
    c = where[3]
    squares = jnp.zeros((32, 128), F32)
    for block in range(16):
        values = tokens[:, block * BLK : (block + 1) * BLK].astype(F32)
        values = values * values
        for lane in range(4):
            squares += values[:, lane * 128 : (lane + 1) * 128]
    for block in range(8):
        col = pl.multiple_of((block * NC + 1 - c) * BLK, BLK)
        send[:, block * BLK : (block + 1) * BLK] = tokens[:, pl.ds(col, BLK)]
    inv = lax.rsqrt(jnp.sum(squares, axis=-1, keepdims=True) / 8192.0 + 1e-05)
    inverse[...] = jnp.broadcast_to(inv, (32, 128))
    kg = (key_grad[...].astype(F32) * inv).astype(BF)
    scaled[...] = kg
    send[:, 4096:] = kg


def partial_kernel(where, tok_own, tok_far, kg_own, *refs):
    outs, kgt = refs[:4], refs[4]
    x, c = where[0], where[3]
    y = where[2] * 2 + where[1]
    for side, kg in enumerate((kg_own[...], tok_far[:, 4096:])):
        turned = kg.T
        for row in range(16):
            to = (row % 2) * 256 + (row // 2) * 32
            kgt[to : to + 32, side * 256 : side * 256 + 256] = turned[row * 32 : row * 32 + 32, :]
    for step in range(4):
        to_x, to_y = (x + step) % NX, (y + step) % 4
        for rh in range(2):
            for ch in range(2):
                row = jnp.where(c == 0, rh, to_y % 2)
                block = jnp.where(c == 0, ch * NX + to_x, (to_y // 2) * NX + rh * 2 + ch)
                left = kgt[pl.ds(pl.multiple_of(row * 256, 256), 256), :]
                own_col = pl.multiple_of((block * NC + c) * BLK, BLK)
                far_col = pl.multiple_of(block * BLK, BLK)
                value = jnp.dot(
                    left[:, :256], tok_own[:, pl.ds(own_col, BLK)], preferred_element_type=F32
                ) + jnp.dot(
                    left[:, 256:], tok_far[:, pl.ds(far_col, BLK)], preferred_element_type=F32
                )
                outs[step][rh * 256 : rh * 256 + 256, ch * BLK : ch * BLK + BLK] = value.astype(BF)


def add(parts, rows, cols):
    out = parts[0][rows, cols].astype(F32)
    for part in parts[1:]:
        out = out + part[rows, cols].astype(F32)
    return out.astype(BF)


def cut_kernel(where, *refs):
    parts, outs = refs[:4], refs[4:]
    c = where[3]
    for step in range(4):
        to_x, to_y = (where[0] + step) % NX, (where[2] * 2 + where[1] + step) % 4
        row = jnp.where(c == 0, to_y % 2, to_x // 2)
        col = jnp.where(c == 0, to_y // 2, to_x % 2)
        outs[step][...] = add(
            parts, pl.ds(pl.multiple_of(row * 256, 256), 256), pl.ds(pl.multiple_of(col * BLK, BLK), BLK)
        )


def sum_kernel(where, *refs):
    refs[4][...] = add(refs[:4], slice(None), slice(None))


def end_kernel(where, gain, parts, out):
    total = jnp.sum(parts[...].astype(F32), axis=0)
    out[...] = (total * gain[pl.ds(where[5], 1), :]).T


def pick_kernel(where, pair, rest, first, out):
    @pl.when(where[3] == 0)
    def _():
        out[...] = rest[...]

    @pl.when(where[3] != 0)
    def _():
        out[...] = pair[...]


def order_kernel(where, pair, rest, got_1, got_2, got_3, up, down):
    up[:BLK, :] = pair[...]

    @pl.when(where[3] == 0)
    def _():
        up[BLK:, :] = rest[...]
        down[:BLK, :] = got_1[...]
        down[BLK:, :] = got_2[...]

    @pl.when(where[3] != 0)
    def _():
        up[BLK:, :] = got_1[...]
        down[:BLK, :] = got_2[...]
        down[BLK:, :] = got_3[...]


def project_kernel(where, tok_own, tok_far, kg_own, *refs):
    pieces, (key_own, key_far, grad_own, grad_far) = refs[:4], refs[-4:]
    x, yh, c, z = where[0], where[2], where[3], where[4]
    key_own[...] = jnp.zeros_like(key_own)
    key_far[...] = jnp.zeros_like(key_far)
    for index in range(16):
        entry = index % 8
        hop = jnp.where(c == 0, entry % 4, entry // 2)
        flip = jnp.where(c == 0, entry // 4, entry % 2)
        block = (yh + flip) % NYH * NX + (x + NX - hop) % NX
        offset = (z + index // 8) % 2 * HALF
        own_col = pl.multiple_of((block * NC + c) * BLK + offset, HALF)
        far_col = pl.multiple_of(block * BLK + offset, HALF)
        weight = pieces[index // 4][(entry % 4) * HALF : (entry % 4 + 1) * HALF, :]
        key_own[...] += jnp.dot(
            tok_own[:, pl.ds(own_col, HALF)], weight, preferred_element_type=F32
        )
        key_far[...] += jnp.dot(
            tok_far[:, pl.ds(far_col, HALF)], weight, preferred_element_type=F32
        )
        for kg, grad in ((kg_own[...], grad_own), (tok_far[:, 4096:], grad_far)):
            grad[:, pl.ds(far_col, HALF)] = lax.dot_general(
                kg, weight, COLS, preferred_element_type=F32
            ).astype(BF)


def finish_kernel(
    where, tokens, grad_a, grad_b, key_a, key_b, kg, inverse, after, key_out, token_grad
):
    c = where[3]
    inv = inverse[:, :1]
    key_sum = key_a[...] + key_b[...]
    key_out[...] = (key_sum * inv).astype(BF)
    dotted = jnp.sum(kg[...].astype(F32) * key_sum, axis=-1, keepdims=True) / 8192.0
    slope = inv * inv * inv * dotted
    for block in range(NYH * NX):
        for refs, parity in ((grad_a, c), (grad_b, 1 - c)):
            col = pl.multiple_of((block * NC + parity) * BLK, BLK)
            part = refs[:, block * BLK : (block + 1) * BLK].astype(F32)
            values = tokens[:, pl.ds(col, BLK)].astype(F32)
            token_grad[:, pl.ds(col, BLK)] = (part - values * slope).astype(BF)


def on_device(tokens, norm_gain, weight_codes, weight_scales, key_grad):
    x, yl, yh, c, z = [lax.axis_index(name) for name in ("x", "yl", "yh", "c", "z")]
    shard = (yh * NX + x) * NC + c
    where = jnp.stack([x, yl, yh, c, z, shard]).astype(jnp.int32)
    gains = norm_gain.reshape(16, BLK)

    weight = call(weight_kernel, "weight", arr((HALF, 512)), dict(in_specs=[smem()] + [vmem()] * 3, out_specs=vmem()), 8, 2**19, 2**20)(
        where, weight_codes, weight_scales, gains
    )
    near = [gather_first(weight, s) for s in (2, 1, 3)]
    pair = jnp.concatenate([weight, near[1]], axis=0)
    rest = jnp.concatenate([near[0], near[2]], axis=0)

    send, kg, inverse = call(
        prep_kernel,
        "prep",
        [arr((256, 4608)), arr((256, 512)), arr((256, 128), F32)],
        dict(
            grid=(8,),
            in_specs=[smem(), rows_spec(8192), rows_spec(512), anywhere()],
            out_specs=[rows_spec(4608), rows_spec(512), rows_spec(128)],
        ),
        8,
        2**22,
        7 * 2**20,
    )(where, tokens, key_grad, weight)
    tok_far = swap_core(send)

    second = call(pick_kernel, "pick", arr((512, 512)), dict(in_specs=[smem()] + [vmem()] * 2 + [anywhere()], out_specs=vmem()), 8, 2**18, 3 * 2**19)(
        where, pair, rest, weight
    )
    got = [gather_second(pair, 1), gather_second(second, 2), gather_second(pair, 3)]
    up, down = call(order_kernel, "order", [arr((1024, 512))] * 2, flat(5, 2), 12, 2**19, 9 * 2**19)(
        where, pair, rest, *got
    )
    pieces = [up, down, along_z(up, 1), along_z(down, -1)]

    outs = call(
        partial_kernel,
        "partial",
        [arr((512, 1024))] * 4,
        flat(3, 4),
        20,
        2**31,
        11 * 2**20,
        scratch_shapes=[pltpu.VMEM((512, 512), BF)],
    )(where, tokens, tok_far, kg)
    cuts = call(cut_kernel, "cut", [arr((256, 512))] * 4, flat(4, 4), 8, 2**20, 5 * 2**20)(
        where, outs[0], *[first_axis(outs[s], s) for s in (1, 2, 3)]
    )
    plane = call(sum_kernel, "sum", arr((256, 512)), dict(in_specs=[smem()] + [vmem()] * 4, out_specs=vmem()), 8, 2**19, 5 * 2**18)(
        where, cuts[0], *[second_axis(cuts[s], s) for s in (1, 2, 3)]
    )
    over_z = lax.all_to_all(
        plane.reshape(NZ, 32, BLK), "z", split_axis=0, concat_axis=0, tiled=True
    )
    weight_grad = call(
        end_kernel, "end", arr((BLK, 32), F32), dict(in_specs=[smem()] + [vmem()] * 2, out_specs=vmem()), 8, 2**17, 2**19
    )(where, gains, over_z)

    key_own, key_far, grad_own, grad_far = call(
        project_kernel,
        "project",
        [arr((256, 512), F32)] * 2 + [arr((256, 4096))] * 2,
        flat(7, 4, 1),
        24,
        2**32,
        16 * 2**20,
    )(where, tokens, tok_far, kg, *pieces, cuts[0])
    key_out, token_grad = call(
        finish_kernel,
        "finish",
        [arr((256, 512)), arr((256, 8192))],
        dict(
            grid=(8,),
            in_specs=[smem()]
            + [rows_spec(n) for n in (8192, 4096, 4096, 512, 512, 512, 128)]
            + [anywhere()],
            out_specs=[rows_spec(512), rows_spec(8192)],
        ),
        8,
        2**23,
        13 * 2**20,
    )(where, tokens, grad_own, swap_core(grad_far), key_own, swap_core(key_far), key_grad, inverse, plane)
    return key_out, token_grad, weight_grad


def solution(mesh):
    fine = Mesh(np.asarray(mesh.devices).reshape(SIZES), AXES)
    outer, inner = ("z", "yl"), ("yh", "x", "c")
    in_specs = (P(outer + inner, None), P(), P(inner, None), P(inner, None), P(outer + inner, None))
    out_specs = (P(outer + inner, None), P(outer + inner, None), P(inner, outer))
    return jax.shard_map(
        on_device, mesh=fine, in_specs=in_specs, out_specs=out_specs, check_vma=False
    )
```

```python
import functools

import jax
import jax.numpy as jnp
import numpy as np
from jax import lax
from jax.experimental import pallas as pl
from jax.experimental.pallas import tpu as pltpu
from jax.sharding import Mesh, PartitionSpec as P

BF, F32 = jnp.bfloat16, jnp.float32
NZ, NYL, NYH, NX, NC = 8, 2, 2, 4, 2
AXES = ("z", "yl", "yh", "x", "c")
SIZES = (NZ, NYL, NYH, NX, NC)
BLK, HALF = 512, 256
COLS = (((1,), (1,)), ((), ()))


def permute(array, target):
    pairs = []
    for flat_id in range(256):
        z, yl, yh, x, c = np.unravel_index(flat_id, SIZES)
        to = target(z, yh * 2 + yl, x, c)
        if to is not None:
            z, y, x, c = to[0] % NZ, to[1] % 4, to[2] % NX, to[3] % NC
            pairs.append((flat_id, int(np.ravel_multi_index((z, y % 2, y // 2, x, c), SIZES))))
    return lax.ppermute(array, AXES, pairs)


def swap_core(array):
    return permute(array, lambda z, y, x, c: (z, y, x, c + 1))


def first_axis(array, step):
    return permute(
        array, lambda z, y, x, c: (z, y, x + step, c) if c == 0 else (z, y + step, x, c)
    )


def second_axis(array, step):
    return permute(
        array, lambda z, y, x, c: (z, y + step, x, c) if c == 0 else (z, y, x + step, c)
    )


def gather_first(array, step):
    def target(z, y, x, c):
        if c == 0:
            return z, y, x + step, c
        return z, y + (2 if step != 2 else 0), x + (2 if step != 1 else 0), c

    return permute(array, target)


def gather_second(array, step):
    def target(z, y, x, c):
        return (z, y + 2, x, c) if c == 0 else (z, y, x + step, c)

    return permute(array, target)


def along_z(array, step):
    return permute(array, lambda z, y, x, c: (z + step, y, x, c))


MARK = jax.ShapeDtypeStruct((8, 128), F32)


def vmem():
    return pl.BlockSpec(memory_space=pltpu.VMEM)


def smem():
    return pl.BlockSpec(memory_space=pltpu.SMEM)


def anywhere():
    return pl.BlockSpec(memory_space=pl.ANY)


def call(kernel, name, outs, grid_args, limit, flops, size, **kw):
    return pl.pallas_call(
        kernel,
        name=name,
        out_shape=outs,
        compiler_params=pltpu.CompilerParams(vmem_limit_bytes=limit * 2**20),
        cost_estimate=pl.CostEstimate(flops=flops, bytes_accessed=size, transcendentals=0),
        **grid_args,
        **kw,
    )


def arr(shape, dtype=BF):
    return jax.ShapeDtypeStruct(shape, dtype)


def flat(inputs, outputs, unused=0):
    return dict(
        in_specs=[smem()] + [vmem()] * inputs + [anywhere()] * unused,
        out_specs=[vmem()] * outputs,
    )


def rows_spec(cols):
    return pl.BlockSpec((64, cols), lambda r: (r, 0))


def weight_kernel(where, codes, scales, gain, out):
    half = where[4] % 2
    column = jnp.broadcast_to(gain[...], (8, HALF)).T[:, :1]
    for group in range(2):
        rows = slice(group * 128, group * 128 + 128)
        values = codes[rows, :].astype(F32) * scales[pl.ds(half * 2 + group, 1), :]
        out[rows, :] = (values * column[rows]).astype(BF)


def prep_kernel(where, tokens, key_grad, after, send, keep, scaled, inverse):
    c = where[3]
    squares = jnp.zeros((64, 128), F32)
    for block in range(16):
        values = tokens[:, block * BLK : (block + 1) * BLK].astype(F32)
        values = values * values
        for lane in range(4):
            squares += values[:, lane * 128 : (lane + 1) * 128]
    for block in range(8):
        col = pl.multiple_of((block * NC + 1 - c) * BLK, BLK)
        send[:, block * BLK : (block + 1) * BLK] = tokens[:, pl.ds(col, BLK)]
        col = pl.multiple_of((block * NC + c) * BLK, BLK)
        keep[:, block * BLK : (block + 1) * BLK] = tokens[:, pl.ds(col, BLK)]
    inv = lax.rsqrt(jnp.sum(squares, axis=-1, keepdims=True) / 8192.0 + 1e-05)
    inverse[...] = jnp.broadcast_to(inv, (64, 128))
    kg = (key_grad[...].astype(F32) * inv).astype(BF)
    scaled[...] = kg
    send[:, 4096:] = kg


def partial_kernel(where, tok_own, tok_far, kg_own, *refs):
    outs, mark, kgt = refs[:4], refs[4], refs[5]
    mark[...] = jnp.zeros_like(mark)
    x, c = where[0], where[3]
    y = where[2] * 2 + where[1]
    for side, kg in enumerate((kg_own[...], tok_far[:, 4096:])):
        turned = kg.T
        for row in range(16):
            to = (row % 2) * 256 + (row // 2) * 32
            kgt[to : to + 32, side * 256 : side * 256 + 256] = turned[row * 32 : row * 32 + 32, :]
    for step in range(4):
        to_x, to_y = (x + step) % NX, (y + step) % 4
        for rh in range(2):
            for ch in range(2):
                row = jnp.where(c == 0, rh, to_y % 2)
                block = jnp.where(c == 0, ch * NX + to_x, (to_y // 2) * NX + rh * 2 + ch)
                left = kgt[pl.ds(pl.multiple_of(row * 256, 256), 256), :]
                cols = pl.ds(pl.multiple_of(block * BLK, BLK), BLK)
                value = jnp.dot(
                    left[:, :256], tok_own[:, cols], preferred_element_type=F32
                ) + jnp.dot(left[:, 256:], tok_far[:, cols], preferred_element_type=F32)
                outs[step][rh * 256 : rh * 256 + 256, ch * BLK : ch * BLK + BLK] = value.astype(BF)


def add(parts, rows, cols):
    out = parts[0][rows, cols].astype(F32)
    for part in parts[1:]:
        out = out + part[rows, cols].astype(F32)
    return out.astype(BF)


def cut_kernel(where, *refs):
    parts, outs = refs[:4], refs[4:]
    c = where[3]
    for step in range(4):
        to_x, to_y = (where[0] + step) % NX, (where[2] * 2 + where[1] + step) % 4
        row = jnp.where(c == 0, to_y % 2, to_x // 2)
        col = jnp.where(c == 0, to_y // 2, to_x % 2)
        outs[step][...] = add(
            parts, pl.ds(pl.multiple_of(row * 256, 256), 256), pl.ds(pl.multiple_of(col * BLK, BLK), BLK)
        )


def sum_kernel(where, *refs):
    refs[4][...] = add(refs[:4], slice(None), slice(None))


def end_kernel(where, gain, parts, after, out):
    out[...] = jnp.sum(parts[...].astype(F32), axis=0) * gain[...]


def pick_kernel(where, weight, near_1, near_2, near_3, after, pair, rest, second):
    pair[:HALF, :] = weight[...]
    pair[HALF:, :] = near_1[...]
    rest[:HALF, :] = near_2[...]
    rest[HALF:, :] = near_3[...]

    @pl.when(where[3] == 0)
    def _():
        second[...] = rest[...]

    @pl.when(where[3] != 0)
    def _():
        second[...] = pair[...]


def order_kernel(where, pair, rest, got_1, got_2, up, down):
    up[:BLK, :] = pair[...]
    down[BLK:, :] = got_2[...]

    @pl.when(where[3] == 0)
    def _():
        up[BLK:, :] = rest[...]
        down[:BLK, :] = got_1[...]

    @pl.when(where[3] != 0)
    def _():
        up[BLK:, :] = got_1[...]
        down[:BLK, :] = rest[...]


def project_kernel(other, where, tok_own, tok_far, kg_own, up, down, *refs):
    key_own, key_far, grad_own, grad_far = refs[-4:]
    x, yh, c, z = where[0], where[2], where[3], where[4]
    if other:
        key_own[...] = refs[0][...]
        key_far[...] = refs[1][...]
    else:
        key_own[...] = jnp.zeros_like(key_own)
        key_far[...] = jnp.zeros_like(key_far)
    for entry in range(8):
        hop = jnp.where(c == 0, entry % 4, entry // 2)
        flip = jnp.where(c == 0, entry // 4, entry % 2)
        block = (yh + flip) % NYH * NX + (x + NX - hop) % NX
        cols = pl.ds(pl.multiple_of(block * BLK + (z + other) % 2 * HALF, HALF), HALF)
        to = pl.ds(pl.multiple_of(block * HALF, HALF), HALF)
        weight = (up, down)[entry // 4][(entry % 4) * HALF : (entry % 4 + 1) * HALF, :]
        key_own[...] += jnp.dot(tok_own[:, cols], weight, preferred_element_type=F32)
        key_far[...] += jnp.dot(tok_far[:, cols], weight, preferred_element_type=F32)
        for kg, grad in ((kg_own[...], grad_own), (tok_far[:, 4096:], grad_far)):
            grad[:, to] = lax.dot_general(kg, weight, COLS, preferred_element_type=F32).astype(BF)


def finish_kernel(where, tokens, *refs):
    grads, (key_a, key_b, kg, inverse, key_out, token_grad, mark) = refs[:4], refs[4:]
    mark[...] = jnp.zeros_like(mark)
    c, z = where[3], where[4]
    inv = inverse[:, :1]
    key_sum = key_a[...] + key_b[...]
    key_out[...] = (key_sum * inv).astype(BF)
    dotted = jnp.sum(kg[...].astype(F32) * key_sum, axis=-1, keepdims=True) / 8192.0
    slope = inv * inv * inv * dotted
    for block in range(NYH * NX):
        for index, grad in enumerate(grads):
            parity, half = (c + index // 2) % 2, (z + index) % 2
            cols = pl.ds(pl.multiple_of((block * NC + parity) * BLK + half * HALF, HALF), HALF)
            part = grad[:, block * HALF : (block + 1) * HALF].astype(F32)
            token_grad[:, cols] = (part - tokens[:, cols].astype(F32) * slope).astype(BF)


def on_device(tokens, norm_gain, weight_codes, weight_scales, key_grad):
    x, yl, yh, c, z = [lax.axis_index(name) for name in ("x", "yl", "yh", "c", "z")]
    shard = (yh * NX + x) * NC + c
    where = jnp.stack([x, yl, yh, c, z, shard]).astype(jnp.int32)
    tokens, key_grad, weight_codes, weight_scales, gains = [
        pltpu.with_memory_space_constraint(array, pltpu.HBM)
        for array in (tokens, key_grad, weight_codes, weight_scales, norm_gain.reshape(1, 8192))
    ]

    weight = call(
        weight_kernel,
        "weight",
        arr((HALF, 512)),
        dict(
            grid_spec=pltpu.PrefetchScalarGridSpec(
                num_scalar_prefetch=1,
                grid=(1,),
                in_specs=[
                    pl.BlockSpec((HALF, 512), lambda i, w: (w[4] % 2, 0)),
                    pl.BlockSpec((4, 512), lambda i, w: (0, 0)),
                    pl.BlockSpec((1, HALF), lambda i, w: (0, w[5] * 2 + w[4] % 2)),
                ],
                out_specs=pl.BlockSpec((HALF, 512), lambda i, w: (0, 0)),
            )
        ),
        8,
        2**19,
        2**20,
    )(where, weight_codes, weight_scales, gains)
    near = [gather_first(weight, s) for s in (1, 2, 3)]

    send, keep, kg, inverse = call(
        prep_kernel,
        "prep",
        [arr((256, 4608)), arr((256, 4096)), arr((256, 512)), arr((256, 128), F32)],
        dict(
            grid=(4,),
            in_specs=[smem(), rows_spec(8192), rows_spec(512), anywhere()],
            out_specs=[rows_spec(4608), rows_spec(4096), rows_spec(512), rows_spec(128)],
        ),
        14,
        2**22,
        9 * 2**20,
    )(where, tokens, key_grad, weight)
    tok_far = swap_core(send)

    *outs, partial_mark = call(
        partial_kernel,
        "partial",
        [arr((512, 1024))] * 4 + [MARK],
        flat(3, 5),
        16,
        2**31,
        9 * 2**20,
        scratch_shapes=[pltpu.VMEM((512, 512), BF)],
    )(where, keep, tok_far, kg)
    outs_here = [first_axis(outs[s], s) for s in (1, 2, 3)]

    pair, rest, second = call(
        pick_kernel, "pick", [arr((512, 512))] * 3, flat(4, 3, 1), 8, 2**18, 3 * 2**20
    )(where, weight, *near, partial_mark)
    got = [gather_second(pair, 1), gather_second(second, 3)]
    up, down = call(
        order_kernel, "order", [arr((1024, 512))] * 2, flat(4, 2), 12, 2**19, 9 * 2**19
    )(where, pair, rest, *got)

    cuts = call(cut_kernel, "cut", [arr((256, 512))] * 4, flat(4, 4), 10, 2**20, 5 * 2**20)(
        where, outs[0], *outs_here
    )
    crossed = [second_axis(cuts[s], s) for s in (1, 2, 3)]

    def project(other, *operands, unused=0):
        return call(
            functools.partial(project_kernel, other),
            "project",
            [arr((256, 512), F32)] * 2 + [arr((256, 2048))] * 2,
            flat(len(operands) - unused, 4, unused),
            16,
            2**31,
            10 * 2**20,
        )(where, *operands)

    key_1, key_far_1, grad_1, grad_far_1 = project(0, keep, tok_far, kg, up, down)
    key_2, key_far_2, grad_2, grad_far_2 = project(
        1, keep, tok_far, kg, along_z(up, 1), along_z(down, -1), key_1, key_far_1, *crossed, unused=3
    )
    plane = call(
        sum_kernel,
        "sum",
        arr((256, 512)),
        dict(in_specs=[smem()] + [vmem()] * 4, out_specs=vmem()),
        8,
        2**19,
        5 * 2**18,
    )(where, cuts[0], *crossed)
    over_z = lax.all_to_all(
        plane.reshape(NZ, 32, BLK), "z", split_axis=0, concat_axis=0, tiled=True
    )
    key_out, token_grad, finish_mark = call(
        finish_kernel,
        "finish",
        [arr((256, 512)), arr((256, 8192)), MARK],
        dict(
            grid=(4,),
            in_specs=[smem(), rows_spec(8192)]
            + [rows_spec(2048)] * 4
            + [rows_spec(n) for n in (512, 512, 512, 128)],
            out_specs=[rows_spec(512), rows_spec(8192), pl.BlockSpec((8, 128), lambda r: (0, 0))],
        ),
        14,
        2**23,
        13 * 2**20,
    )(
        where,
        tokens,
        grad_1,
        grad_2,
        swap_core(grad_far_1),
        swap_core(grad_far_2),
        key_2,
        swap_core(key_far_2),
        key_grad,
        inverse,
    )
    weight_grad = call(
        end_kernel,
        "end",
        arr((32, BLK), F32),
        dict(
            grid_spec=pltpu.PrefetchScalarGridSpec(
                num_scalar_prefetch=1,
                grid=(1,),
                in_specs=[
                    pl.BlockSpec((1, BLK), lambda i, w: (0, w[5])),
                    pl.BlockSpec((NZ, 32, BLK), lambda i, w: (0, 0, 0)),
                    anywhere(),
                ],
                out_specs=pl.BlockSpec((32, BLK), lambda i, w: (0, 0)),
            )
        ),
        8,
        2**17,
        2**19,
    )(where, gains, over_z, finish_mark).T
    return key_out, token_grad, weight_grad


def solution(mesh):
    fine = Mesh(np.asarray(mesh.devices).reshape(SIZES), AXES)
    outer, inner = ("z", "yl"), ("yh", "x", "c")
    in_specs = (P(outer + inner, None), P(), P(inner, None), P(inner, None), P(outer + inner, None))
    out_specs = (P(outer + inner, None), P(outer + inner, None), P(inner, outer))
    return jax.shard_map(
        on_device, mesh=fine, in_specs=in_specs, out_specs=out_specs, check_vma=False
    )
```

```python
import functools

import jax
import jax.numpy as jnp
import numpy as np
from jax import lax
from jax.experimental import pallas as pl
from jax.experimental.pallas import tpu as pltpu
from jax.sharding import Mesh, PartitionSpec as P

BF, F32 = jnp.bfloat16, jnp.float32
NZ, NYL, NYH, NX, NC = 8, 2, 2, 4, 2
AXES = ("z", "yl", "yh", "x", "c")
SIZES = (NZ, NYL, NYH, NX, NC)
BLK, HALF = 512, 256
COLS = (((1,), (1,)), ((), ()))


def permute(array, target):
    pairs = []
    for flat_id in range(256):
        z, yl, yh, x, c = np.unravel_index(flat_id, SIZES)
        to = target(z, yh * 2 + yl, x, c)
        if to is not None:
            z, y, x, c = to[0] % NZ, to[1] % 4, to[2] % NX, to[3] % NC
            pairs.append((flat_id, int(np.ravel_multi_index((z, y % 2, y // 2, x, c), SIZES))))
    return lax.ppermute(array, AXES, pairs)


def swap_core(array):
    return permute(array, lambda z, y, x, c: (z, y, x, c + 1))


def first_axis(array, step):
    return permute(
        array, lambda z, y, x, c: (z, y, x + step, c) if c == 0 else (z, y + step, x, c)
    )


def second_axis(array, step):
    return permute(
        array, lambda z, y, x, c: (z, y + step, x, c) if c == 0 else (z, y, x + step, c)
    )


ORIGIN = (
    ((0, 0), (1, 0), (2, 0), (3, 0), (0, 1), (1, 1), (2, 1), (3, 1)),
    ((0, 0), (0, 1), (1, 0), (3, 1), (1, 1), (2, 0), (3, 0), (2, 1)),
)


def block_of(where, core, entry):
    hops = [ORIGIN[core_id][entry] for core_id in range(2)]
    hop = jnp.where(core == 0, hops[0][0], hops[1][0])
    flip = jnp.where(core == 0, hops[0][1], hops[1][1])
    return (where[2] + flip) % NYH * NX + (where[0] + NX - hop) % NX


def gather_first(array, step):
    def target(z, y, x, c):
        if c == 0:
            return z, y, x + step, c
        return ((z, y + 2, x, c), (z, y, x + 1, c), (z, y + 2, x - 1, c))[step - 1]

    return permute(array, target)


def gather_second(array, step):
    def target(z, y, x, c):
        return (z, y + 2, x, c) if c == 0 else (z, y, x + step, c)

    return permute(array, target)


def along_z(array, step):
    return permute(array, lambda z, y, x, c: (z + step, y, x, c))


COSTLY = ("sum", "finish")
MARK = jax.ShapeDtypeStruct((8, 128), F32)


def vmem():
    return pl.BlockSpec(memory_space=pltpu.VMEM)


def smem():
    return pl.BlockSpec(memory_space=pltpu.SMEM)


def anywhere():
    return pl.BlockSpec(memory_space=pl.ANY)


def call(kernel, name, outs, grid_args, limit, flops, size, **kw):
    return pl.pallas_call(
        kernel,
        name=name,
        out_shape=outs,
        compiler_params=pltpu.CompilerParams(vmem_limit_bytes=limit * 2**20),
        cost_estimate=pl.CostEstimate(
            flops=flops if name in COSTLY else 1, bytes_accessed=size if name in COSTLY else 1, transcendentals=0
        ),
        **grid_args,
        **kw,
    )


def arr(shape, dtype=BF):
    return jax.ShapeDtypeStruct(shape, dtype)


def flat(inputs, outputs, unused=0):
    return dict(
        in_specs=[smem()] + [vmem()] * inputs + [anywhere()] * unused,
        out_specs=[vmem()] * outputs,
    )


def rows_spec(cols):
    return pl.BlockSpec((64, cols), lambda r: (r, 0))


def prep_kernel(
    where, tokens, key_grad, codes, scales, gain, send, keep, scaled, inverse, weight, other, row
):
    @pl.when(pl.program_id(0) == 0)
    def _():
        row[...] = jnp.broadcast_to(gain[...], (8, BLK))
        column = jnp.broadcast_to(gain[...], (8, BLK)).T[:, :1]
        for group in range(4):
            rows = slice(group * 128, group * 128 + 128)
            to = slice((group % 2) * 128, (group % 2) * 128 + 128)
            part = codes[rows, :].astype(F32) * scales[group : group + 1, :]
            part = (part * column[rows]).astype(BF)

            @pl.when(where[4] % 2 == group // 2)
            def _():
                weight[to, :] = part

            @pl.when(where[4] % 2 != group // 2)
            def _():
                other[to, :] = part

    c = where[3]
    squares = jnp.zeros((64, 128), F32)
    for block in range(16):
        values = tokens[:, block * BLK : (block + 1) * BLK].astype(F32)
        values = values * values
        for lane in range(4):
            squares += values[:, lane * 128 : (lane + 1) * 128]
    for block in range(8):
        col = pl.multiple_of((block * NC + 1 - c) * BLK, BLK)
        send[:, block * BLK : (block + 1) * BLK] = tokens[:, pl.ds(col, BLK)]
        col = pl.multiple_of((block * NC + c) * BLK, BLK)
        keep[:, block * BLK : (block + 1) * BLK] = tokens[:, pl.ds(col, BLK)]
    inv = lax.rsqrt(jnp.sum(squares, axis=-1, keepdims=True) / 8192.0 + 1e-05)
    inverse[...] = jnp.broadcast_to(inv, (64, 128))
    kg = (key_grad[...].astype(F32) * inv).astype(BF)
    scaled[...] = kg
    send[:, 4096:] = kg


def partial_kernel(steps, where, tok_own, tok_far, kg_own, *refs):
    *outs, mark, kgt = refs
    mark[...] = jnp.zeros_like(mark)
    x, c = where[0], where[3]
    y = where[2] * 2 + where[1]
    for side, kg in enumerate((kg_own[...], tok_far[:, 4096:])):
        turned = kg.T
        for row in range(16):
            to = (row % 2) * 256 + (row // 2) * 32
            kgt[to : to + 32, side * 256 : side * 256 + 256] = turned[row * 32 : row * 32 + 32, :]
    for step, out in zip(steps, outs):
        to_x, to_y = (x + step) % NX, (y + step) % 4
        for rh in range(2):
            for ch in range(2):
                row = jnp.where(c == 0, rh, to_y % 2)
                block = jnp.where(c == 0, ch * NX + to_x, (to_y // 2) * NX + rh * 2 + ch)
                left = kgt[pl.ds(pl.multiple_of(row * 256, 256), 256), :]
                cols = pl.ds(pl.multiple_of(block * BLK, BLK), BLK)
                value = jnp.dot(
                    left[:, :256], tok_own[:, cols], preferred_element_type=F32
                ) + jnp.dot(left[:, 256:], tok_far[:, cols], preferred_element_type=F32)
                out[rh * 256 : rh * 256 + 256, ch * BLK : ch * BLK + BLK] = value.astype(BF)


def add(parts, rows, cols):
    out = parts[0][rows, cols].astype(F32)
    for part in parts[1:]:
        out = out + part[rows, cols].astype(F32)
    return out.astype(BF)


def cut_kernel(where, *refs):
    parts, outs, mark = refs[:4], refs[-5:-1], refs[-1]
    mark[...] = jnp.zeros_like(mark)
    c = where[3]
    for step in range(4):
        to_x, to_y = (where[0] + step) % NX, (where[2] * 2 + where[1] + step) % 4
        row = jnp.where(c == 0, to_y % 2, to_x // 2)
        col = jnp.where(c == 0, to_y // 2, to_x % 2)
        outs[step][...] = add(
            parts, pl.ds(pl.multiple_of(row * 256, 256), 256), pl.ds(pl.multiple_of(col * BLK, BLK), BLK)
        )


def sum_kernel(where, *refs):
    refs[5][...] = add(refs[:4], slice(None), slice(None))


def end_kernel(where, gain, parts, after, out):
    out[...] = jnp.sum(parts[...].astype(F32), axis=0) * gain[:1, :]


def pick_kernel(where, weight, near_1, near_2, near_3, after, rows, send_1, send_2):
    rows[:HALF, :] = near_1[...]
    rows[HALF:BLK, :] = near_2[...]
    rows[BLK:, :] = near_3[...]
    send_2[HALF:, :] = near_3[...]

    @pl.when(where[3] == 0)
    def _():
        send_1[:HALF, :] = weight[...]
        send_1[HALF:, :] = near_1[...]
        send_2[:HALF, :] = near_2[...]

    @pl.when(where[3] != 0)
    def _():
        send_1[:HALF, :] = near_1[...]
        send_1[HALF:, :] = near_2[...]
        send_2[:HALF, :] = weight[...]


def relay_kernel(where, source, after, out):
    out[...] = source[...]


def project_kernel(first, where, tok_own, tok_far, kg_own, *refs):
    key_own, key_far, grad_own, grad_far, mark = refs[-5:]
    mark[...] = jnp.zeros_like(mark)
    if first == 0:
        key_own[...] = jnp.zeros_like(key_own)
        key_far[...] = jnp.zeros_like(key_far)
    else:
        key_own[...] = refs[4][...]
        key_far[...] = refs[5][...]
    pieces = [ref.at[row : row + HALF, :] for ref in refs[:4] for row in range(0, ref.shape[0], HALF)]
    if first == 0:
        pieces = [pieces[index] for index in (0, 2, 3, 4, 1, 5, 6, 7)]
    for index, piece in enumerate(pieces):
        half = (where[4] + index // 4) % 2
        block = block_of(where, where[3], first + index % 4)
        cols = pl.ds(pl.multiple_of(block * BLK + half * HALF, HALF), HALF)
        to = slice(index * HALF, (index + 1) * HALF)
        weight = piece[...]
        key_own[...] += jnp.dot(tok_own[:, cols], weight, preferred_element_type=F32)
        key_far[...] += jnp.dot(tok_far[:, cols], weight, preferred_element_type=F32)
        for kg, grad in ((kg_own[...], grad_own), (tok_far[:, 4096:], grad_far)):
            grad[:, to] = lax.dot_general(kg, weight, COLS, preferred_element_type=F32).astype(BF)


def finish_kernel(where, tokens, *refs):
    grads, (key_a, key_b, kg, inverse, key_out, token_grad, mark) = refs[:4], refs[4:]
    mark[...] = jnp.zeros_like(mark)
    c, z = where[3], where[4]
    inv = inverse[:, :1]
    key_sum = key_a[...] + key_b[...]
    key_out[...] = (key_sum * inv).astype(BF)
    dotted = jnp.sum(kg[...].astype(F32) * key_sum, axis=-1, keepdims=True) / 8192.0
    slope = inv * inv * inv * dotted
    for source, grad in enumerate(grads):
        core = (c + source // 2) % 2
        for index in range(8):
            half = (z + index // 4) % 2
            block = block_of(where, core, (source % 2) * 4 + index % 4)
            cols = pl.ds(pl.multiple_of((block * NC + core) * BLK + half * HALF, HALF), HALF)
            part = grad[:, index * HALF : (index + 1) * HALF].astype(F32)
            token_grad[:, cols] = (part - tokens[:, cols].astype(F32) * slope).astype(BF)


def on_device(tokens, norm_gain, weight_codes, weight_scales, key_grad):
    x, yl, yh, c, z = [lax.axis_index(name) for name in ("x", "yl", "yh", "c", "z")]
    shard = (yh * NX + x) * NC + c
    where = jnp.stack([x, yl, yh, c, z, shard]).astype(jnp.int32)
    tokens, key_grad, weight_codes, weight_scales, gains = [
        pltpu.with_memory_space_constraint(array, pltpu.HBM)
        for array in (tokens, key_grad, weight_codes, weight_scales, norm_gain.reshape(1, 8192))
    ]

    def fixed(rows, cols):
        return pl.BlockSpec((rows, cols), lambda r, w: (0, 0))

    def moving(cols):
        return pl.BlockSpec((64, cols), lambda r, w: (r, 0))

    send, keep, kg, inverse, weight, weight_other, gain_row = call(
        prep_kernel,
        "prep",
        [arr((256, 4608)), arr((256, 4096)), arr((256, 512)), arr((256, 128), F32)]
        + [arr((HALF, 512))] * 2
        + [arr((8, BLK), F32)],
        dict(
            grid_spec=pltpu.PrefetchScalarGridSpec(
                num_scalar_prefetch=1,
                grid=(4,),
                in_specs=[
                    moving(8192),
                    moving(512),
                    fixed(BLK, 512),
                    fixed(4, 512),
                    pl.BlockSpec((1, BLK), lambda r, w: (0, w[5])),
                ],
                out_specs=[moving(4608), moving(4096), moving(512), moving(128)]
                + [fixed(HALF, 512)] * 2
                + [fixed(8, BLK)],
            )
        ),
        14,
        2**22,
        9 * 2**20,
    )(where, tokens, key_grad, weight_codes, weight_scales, gains)
    near = [gather_first(weight, s) for s in (1, 2, 3)]
    tok_far = swap_core(send)

    *parts, partial_mark = call(
        functools.partial(partial_kernel, range(4)),
        "partial",
        [arr((512, 1024))] * 4 + [MARK],
        flat(3, 5),
        16,
        2**31,
        9 * 2**20,
        scratch_shapes=[pltpu.VMEM((512, 512), BF)],
    )(where, keep, tok_far, kg)

    near_rows, send_1, send_2 = call(
        pick_kernel,
        "pick",
        [arr((768, 512)), arr((512, 512)), arr((512, 512))],
        flat(4, 3, 1),
        8,
        2**18,
        3 * 2**20,
    )(where, weight, *near, partial_mark)
    got_1, got_2 = gather_second(send_1, 1), gather_second(send_2, 3)


    def project(first, *operands, unused=0):
        return call(
            functools.partial(project_kernel, first),
            "project",
            [arr((256, 512), F32)] * 2 + [arr((256, 2048))] * 2 + [MARK],
            flat(len(operands) - unused, 5, unused),
            16,
            2**31,
            10 * 2**20,
        )(where, *operands)

    key_1, key_far_1, grad_1, grad_far_1, early_mark = project(
        0, keep, tok_far, kg, weight, weight_other, near_rows, along_z(near_rows, 1)
    )
    relayed = call(
        relay_kernel,
        "relay",
        arr((512, 512)),
        dict(in_specs=[smem(), vmem(), anywhere()], out_specs=vmem()),
        8,
        2**18,
        2**20,
    )(where, got_2, early_mark)
    *cuts, cut_mark = call(cut_kernel, "cut", [arr((256, 512))] * 4 + [MARK], flat(4, 5, 1), 10, 2**20, 5 * 2**20)(
        where,
        parts[0],
        first_axis(parts[1], 1),
        first_axis(parts[2], 2),
        first_axis(parts[3], 3),
        early_mark,
    )
    crossed = [second_axis(cuts[s], s) for s in (1, 2, 3)]
    key_2, key_far_2, grad_2, grad_far_2, project_mark = project(
        4,
        keep,
        tok_far,
        kg,
        got_1,
        got_2,
        along_z(got_1, 1),
        along_z(relayed, -1),
        key_1,
        key_far_1,
        cut_mark,
        unused=1,
    )

    plane = call(
        sum_kernel,
        "sum",
        arr((256, 512)),
        dict(in_specs=[smem()] + [vmem()] * 4 + [anywhere()], out_specs=vmem()),
        8,
        14 * 10**9,
        5 * 2**18,
    )(where, cuts[0], *crossed, project_mark)
    over_z = lax.all_to_all(
        plane.reshape(NZ, 32, BLK), "z", split_axis=0, concat_axis=0, tiled=True
    )
    key_out, token_grad, finish_mark = call(
        finish_kernel,
        "finish",
        [arr((256, 512)), arr((256, 8192)), MARK],
        dict(
            grid=(4,),
            in_specs=[smem(), rows_spec(8192)]
            + [rows_spec(2048)] * 4
            + [rows_spec(n) for n in (512, 512, 512, 128)],
            out_specs=[rows_spec(512), rows_spec(8192), pl.BlockSpec((8, 128), lambda r: (0, 0))],
        ),
        14,
        2**23,
        13 * 2**20,
    )(
        where,
        tokens,
        grad_1,
        grad_2,
        swap_core(grad_far_1),
        swap_core(grad_far_2),
        key_2,
        swap_core(key_far_2),
        key_grad,
        inverse,
    )
    weight_grad = call(
        end_kernel,
        "end",
        arr((32, BLK), F32),
        dict(in_specs=[smem(), vmem(), vmem(), anywhere()], out_specs=vmem()),
        8,
        2**17,
        2**19,
    )(where, gain_row, over_z, finish_mark).T
    return key_out, token_grad, weight_grad


def solution(mesh):
    fine = Mesh(np.asarray(mesh.devices).reshape(SIZES), AXES)
    outer, inner = ("z", "yl"), ("yh", "x", "c")
    in_specs = (P(outer + inner, None), P(), P(inner, None), P(inner, None), P(outer + inner, None))
    out_specs = (P(outer + inner, None), P(outer + inner, None), P(inner, outer))
    return jax.shard_map(
        on_device, mesh=fine, in_specs=in_specs, out_specs=out_specs, check_vma=False
    )
```

```python
import functools

import jax
import jax.numpy as jnp
import numpy as np
from jax import lax
from jax.experimental import pallas as pl
from jax.experimental.pallas import tpu as pltpu
from jax.sharding import Mesh, PartitionSpec as P

BF, F32 = jnp.bfloat16, jnp.float32
NZ, NYL, NYH, NX, NC = 8, 2, 2, 4, 2
AXES = ("z", "yl", "yh", "x", "c")
SIZES = (NZ, NYL, NYH, NX, NC)
BLK, HALF = 512, 256
COLS = (((1,), (1,)), ((), ()))


def permute(array, target):
    pairs = []
    for flat_id in range(256):
        z, yl, yh, x, c = np.unravel_index(flat_id, SIZES)
        to = target(z, yh * 2 + yl, x, c)
        if to is not None:
            z, y, x, c = to[0] % NZ, to[1] % 4, to[2] % NX, to[3] % NC
            pairs.append((flat_id, int(np.ravel_multi_index((z, y % 2, y // 2, x, c), SIZES))))
    return lax.ppermute(array, AXES, pairs)


def swap_core(array):
    return permute(array, lambda z, y, x, c: (z, y, x, c + 1))


def first_axis(array, step):
    return permute(
        array, lambda z, y, x, c: (z, y, x + step, c) if c == 0 else (z, y + step, x, c)
    )


def second_axis(array, step):
    return permute(
        array, lambda z, y, x, c: (z, y + step, x, c) if c == 0 else (z, y, x + step, c)
    )


ORIGIN = (
    ((0, 0), (1, 0), (2, 0), (3, 0), (0, 1), (1, 1), (2, 1), (3, 1)),
    ((0, 0), (0, 1), (1, 0), (3, 1), (1, 1), (2, 0), (3, 0), (2, 1)),
)


def block_of(where, core, entry):
    hops = [ORIGIN[core_id][entry] for core_id in range(2)]
    hop = jnp.where(core == 0, hops[0][0], hops[1][0])
    flip = jnp.where(core == 0, hops[0][1], hops[1][1])
    return (where[2] + flip) % NYH * NX + (where[0] + NX - hop) % NX


def gather_first(array, step):
    def target(z, y, x, c):
        if c == 0:
            return z, y, x + step, c
        return ((z, y + 2, x, c), (z, y, x + 1, c), (z, y + 2, x - 1, c))[step - 1]

    return permute(array, target)


def gather_second(array, step):
    def target(z, y, x, c):
        return (z, y + 2, x, c) if c == 0 else (z, y, x + step, c)

    return permute(array, target)


def along_z(array, step):
    return permute(array, lambda z, y, x, c: (z + step, y, x, c))


COSTLY = ("sum", "finish")
MARK = jax.ShapeDtypeStruct((8, 128), F32)


def vmem():
    return pl.BlockSpec(memory_space=pltpu.VMEM)


def smem():
    return pl.BlockSpec(memory_space=pltpu.SMEM)


def anywhere():
    return pl.BlockSpec(memory_space=pl.ANY)


def call(kernel, name, outs, grid_args, limit, flops, size, **kw):
    return pl.pallas_call(
        kernel,
        name=name,
        out_shape=outs,
        compiler_params=pltpu.CompilerParams(vmem_limit_bytes=limit * 2**20),
        cost_estimate=pl.CostEstimate(
            flops=flops if name in COSTLY else 1, bytes_accessed=size if name in COSTLY else 1, transcendentals=0
        ),
        **grid_args,
        **kw,
    )


def arr(shape, dtype=BF):
    return jax.ShapeDtypeStruct(shape, dtype)


def flat(inputs, outputs, unused=0):
    return dict(
        in_specs=[smem()] + [vmem()] * inputs + [anywhere()] * unused,
        out_specs=[vmem()] * outputs,
    )


def rows_spec(cols):
    return pl.BlockSpec((64, cols), lambda r: (r, 0))


def prep_kernel(
    where, tokens, key_grad, codes, scales, gain, send, keep, scaled, inverse, weight, other, row
):
    @pl.when(pl.program_id(0) == 0)
    def _():
        row[...] = jnp.broadcast_to(gain[...], (8, BLK))
        column = jnp.broadcast_to(gain[...], (8, BLK)).T[:, :1]
        for group in range(4):
            rows = slice(group * 128, group * 128 + 128)
            to = slice((group % 2) * 128, (group % 2) * 128 + 128)
            part = codes[rows, :].astype(F32) * scales[group : group + 1, :]
            part = (part * column[rows]).astype(BF)

            @pl.when(where[4] % 2 == group // 2)
            def _():
                weight[to, :] = part

            @pl.when(where[4] % 2 != group // 2)
            def _():
                other[to, :] = part

    c = where[3]
    squares = jnp.zeros((64, 128), F32)
    for block in range(16):
        values = tokens[:, block * BLK : (block + 1) * BLK].astype(F32)
        values = values * values
        for lane in range(4):
            squares += values[:, lane * 128 : (lane + 1) * 128]
    for block in range(8):
        col = pl.multiple_of((block * NC + 1 - c) * BLK, BLK)
        send[:, block * BLK : (block + 1) * BLK] = tokens[:, pl.ds(col, BLK)]
        col = pl.multiple_of((block * NC + c) * BLK, BLK)
        keep[:, block * BLK : (block + 1) * BLK] = tokens[:, pl.ds(col, BLK)]
    inv = lax.rsqrt(jnp.sum(squares, axis=-1, keepdims=True) / 8192.0 + 1e-05)
    inverse[...] = jnp.broadcast_to(inv, (64, 128))
    kg = (key_grad[...].astype(F32) * inv).astype(BF)
    scaled[...] = kg
    send[:, 4096:] = kg


def partial_kernel(steps, where, tok_own, tok_far, kg_own, *refs):
    *outs, mark, kgt = refs
    mark[...] = jnp.zeros_like(mark)
    x, c = where[0], where[3]
    y = where[2] * 2 + where[1]
    for side, kg in enumerate((kg_own[...], tok_far[:, 4096:])):
        turned = kg.T
        for row in range(16):
            to = (row % 2) * 256 + (row // 2) * 32
            kgt[to : to + 32, side * 256 : side * 256 + 256] = turned[row * 32 : row * 32 + 32, :]
    for step, out in zip(steps, outs):
        to_x, to_y = (x + step) % NX, (y + step) % 4
        for rh in range(2):
            for ch in range(2):
                row = jnp.where(c == 0, rh, to_y % 2)
                block = jnp.where(c == 0, ch * NX + to_x, (to_y // 2) * NX + rh * 2 + ch)
                left = kgt[pl.ds(pl.multiple_of(row * 256, 256), 256), :]
                cols = pl.ds(pl.multiple_of(block * BLK, BLK), BLK)
                value = jnp.dot(
                    left[:, :256], tok_own[:, cols], preferred_element_type=F32
                ) + jnp.dot(left[:, 256:], tok_far[:, cols], preferred_element_type=F32)
                out[rh * 256 : rh * 256 + 256, ch * BLK : ch * BLK + BLK] = value.astype(BF)


def add(parts, rows, cols):
    out = parts[0][rows, cols].astype(F32)
    for part in parts[1:]:
        out = out + part[rows, cols].astype(F32)
    return out.astype(BF)


def cut_kernel(where, *refs):
    parts, outs, mark = refs[:4], refs[-5:-1], refs[-1]
    mark[...] = jnp.zeros_like(mark)
    c = where[3]
    for step in range(4):
        to_x, to_y = (where[0] + step) % NX, (where[2] * 2 + where[1] + step) % 4
        row = jnp.where(c == 0, to_y % 2, to_x // 2)
        col = jnp.where(c == 0, to_y // 2, to_x % 2)
        outs[step][...] = add(
            parts, pl.ds(pl.multiple_of(row * 256, 256), 256), pl.ds(pl.multiple_of(col * BLK, BLK), BLK)
        )


def sum_kernel(where, gain, *refs):
    total = refs[0][...].astype(F32)
    for part in refs[1:4]:
        total = total + part[...].astype(F32)
    refs[5][...] = (total * gain[:1, :]).astype(BF)


def end_kernel(where, parts, after, out):
    out[...] = jnp.sum(parts[...].astype(F32), axis=0)


def pick_kernel(where, weight, near_1, near_2, near_3, after, rows, send_1, send_2):
    rows[:HALF, :] = near_1[...]
    rows[HALF:BLK, :] = near_2[...]
    rows[BLK:, :] = near_3[...]
    send_2[HALF:, :] = near_3[...]

    @pl.when(where[3] == 0)
    def _():
        send_1[:HALF, :] = weight[...]
        send_1[HALF:, :] = near_1[...]
        send_2[:HALF, :] = near_2[...]

    @pl.when(where[3] != 0)
    def _():
        send_1[:HALF, :] = near_1[...]
        send_1[HALF:, :] = near_2[...]
        send_2[:HALF, :] = weight[...]


def relay_kernel(where, source, after, out):
    out[...] = source[...]


def project_kernel(first, where, tok_own, tok_far, kg_own, *refs):
    key_own, key_far, grad_own, grad_far, mark = refs[-5:]
    mark[...] = jnp.zeros_like(mark)
    if first == 0:
        key_own[...] = jnp.zeros_like(key_own)
        key_far[...] = jnp.zeros_like(key_far)
    else:
        key_own[...] = refs[4][...]
        key_far[...] = refs[5][...]
    pieces = [ref.at[row : row + HALF, :] for ref in refs[:4] for row in range(0, ref.shape[0], HALF)]
    if first == 0:
        pieces = [pieces[index] for index in (0, 2, 3, 4, 1, 5, 6, 7)]
    for index, piece in enumerate(pieces):
        half = (where[4] + index // 4) % 2
        block = block_of(where, where[3], first + index % 4)
        cols = pl.ds(pl.multiple_of(block * BLK + half * HALF, HALF), HALF)
        to = slice(index * HALF, (index + 1) * HALF)
        weight = piece[...]
        key_own[...] += jnp.dot(tok_own[:, cols], weight, preferred_element_type=F32)
        key_far[...] += jnp.dot(tok_far[:, cols], weight, preferred_element_type=F32)
        for kg, grad in ((kg_own[...], grad_own), (tok_far[:, 4096:], grad_far)):
            grad[:, to] = lax.dot_general(kg, weight, COLS, preferred_element_type=F32).astype(BF)


def finish_kernel(where, tokens, *refs):
    grads, (key_a, key_b, kg, inverse, key_out, token_grad, mark) = refs[:4], refs[4:]
    mark[...] = jnp.zeros_like(mark)
    c, z = where[3], where[4]
    inv = inverse[:, :1]
    key_sum = key_a[...] + key_b[...]
    key_out[...] = (key_sum * inv).astype(BF)
    dotted = jnp.sum(kg[...].astype(F32) * key_sum, axis=-1, keepdims=True) / 8192.0
    slope = inv * inv * inv * dotted
    for source, grad in enumerate(grads):
        core = (c + source // 2) % 2
        for index in range(8):
            half = (z + index // 4) % 2
            block = block_of(where, core, (source % 2) * 4 + index % 4)
            cols = pl.ds(pl.multiple_of((block * NC + core) * BLK + half * HALF, HALF), HALF)
            part = grad[:, index * HALF : (index + 1) * HALF].astype(F32)
            token_grad[:, cols] = (part - tokens[:, cols].astype(F32) * slope).astype(BF)


def on_device(tokens, norm_gain, weight_codes, weight_scales, key_grad):
    x, yl, yh, c, z = [lax.axis_index(name) for name in ("x", "yl", "yh", "c", "z")]
    shard = (yh * NX + x) * NC + c
    where = jnp.stack([x, yl, yh, c, z, shard]).astype(jnp.int32)
    tokens, key_grad, weight_codes, weight_scales, gains = [
        pltpu.with_memory_space_constraint(array, pltpu.HBM)
        for array in (tokens, key_grad, weight_codes, weight_scales, norm_gain.reshape(1, 8192))
    ]

    def fixed(rows, cols):
        return pl.BlockSpec((rows, cols), lambda r, w: (0, 0))

    def moving(cols):
        return pl.BlockSpec((64, cols), lambda r, w: (r, 0))

    send, keep, kg, inverse, weight, weight_other, gain_row = call(
        prep_kernel,
        "prep",
        [arr((256, 4608)), arr((256, 4096)), arr((256, 512)), arr((256, 128), F32)]
        + [arr((HALF, 512))] * 2
        + [arr((8, BLK), F32)],
        dict(
            grid_spec=pltpu.PrefetchScalarGridSpec(
                num_scalar_prefetch=1,
                grid=(4,),
                in_specs=[
                    moving(8192),
                    moving(512),
                    fixed(BLK, 512),
                    fixed(4, 512),
                    pl.BlockSpec((1, BLK), lambda r, w: (0, w[5])),
                ],
                out_specs=[moving(4608), moving(4096), moving(512), moving(128)]
                + [fixed(HALF, 512)] * 2
                + [fixed(8, BLK)],
            )
        ),
        14,
        2**22,
        9 * 2**20,
    )(where, tokens, key_grad, weight_codes, weight_scales, gains)
    near = [gather_first(weight, s) for s in (1, 2, 3)]
    tok_far = swap_core(send)

    *parts, partial_mark = call(
        functools.partial(partial_kernel, range(4)),
        "partial",
        [arr((512, 1024))] * 4 + [MARK],
        flat(3, 5),
        16,
        2**31,
        9 * 2**20,
        scratch_shapes=[pltpu.VMEM((512, 512), BF)],
    )(where, keep, tok_far, kg)

    near_rows, send_1, send_2 = call(
        pick_kernel,
        "pick",
        [arr((768, 512)), arr((512, 512)), arr((512, 512))],
        flat(4, 3, 1),
        8,
        2**18,
        3 * 2**20,
    )(where, weight, *near, partial_mark)
    got_1, got_2 = gather_second(send_1, 1), gather_second(send_2, 3)


    def project(first, *operands, unused=0):
        return call(
            functools.partial(project_kernel, first),
            "project",
            [arr((256, 512), F32)] * 2 + [arr((256, 2048))] * 2 + [MARK],
            flat(len(operands) - unused, 5, unused),
            16,
            2**31,
            10 * 2**20,
        )(where, *operands)

    key_1, key_far_1, grad_1, grad_far_1, early_mark = project(
        0, keep, tok_far, kg, weight, weight_other, near_rows, along_z(near_rows, 1)
    )
    relayed = call(
        relay_kernel,
        "relay",
        arr((512, 512)),
        dict(in_specs=[smem(), vmem(), anywhere()], out_specs=vmem()),
        8,
        2**18,
        2**20,
    )(where, got_2, early_mark)
    *cuts, cut_mark = call(cut_kernel, "cut", [arr((256, 512))] * 4 + [MARK], flat(4, 5, 1), 10, 2**20, 5 * 2**20)(
        where,
        parts[0],
        first_axis(parts[1], 1),
        first_axis(parts[2], 2),
        first_axis(parts[3], 3),
        early_mark,
    )
    crossed = [second_axis(cuts[s], s) for s in (1, 2, 3)]
    key_2, key_far_2, grad_2, grad_far_2, project_mark = project(
        4,
        keep,
        tok_far,
        kg,
        got_1,
        got_2,
        along_z(got_1, 1),
        along_z(relayed, -1),
        key_1,
        key_far_1,
        cut_mark,
        unused=1,
    )

    plane = call(
        sum_kernel,
        "sum",
        arr((256, 512)),
        dict(in_specs=[smem()] + [vmem()] * 5 + [anywhere()], out_specs=vmem()),
        8,
        14 * 10**9,
        5 * 2**18,
    )(where, gain_row, cuts[0], *crossed, project_mark)
    over_z = lax.all_to_all(
        plane.reshape(NZ, 32, BLK), "z", split_axis=0, concat_axis=0, tiled=True
    )
    key_out, token_grad, finish_mark = call(
        finish_kernel,
        "finish",
        [arr((256, 512)), arr((256, 8192)), MARK],
        dict(
            grid=(4,),
            in_specs=[smem(), rows_spec(8192)]
            + [rows_spec(2048)] * 4
            + [rows_spec(n) for n in (512, 512, 512, 128)],
            out_specs=[rows_spec(512), rows_spec(8192), pl.BlockSpec((8, 128), lambda r: (0, 0))],
        ),
        14,
        2**23,
        13 * 2**20,
    )(
        where,
        tokens,
        grad_1,
        grad_2,
        swap_core(grad_far_1),
        swap_core(grad_far_2),
        key_2,
        swap_core(key_far_2),
        key_grad,
        inverse,
    )
    weight_grad = call(
        end_kernel,
        "end",
        arr((32, BLK), F32),
        dict(in_specs=[smem(), vmem(), anywhere()], out_specs=vmem()),
        8,
        2**17,
        2**19,
    )(where, over_z, finish_mark).T
    return key_out, token_grad, weight_grad


def solution(mesh):
    fine = Mesh(np.asarray(mesh.devices).reshape(SIZES), AXES)
    outer, inner = ("z", "yl"), ("yh", "x", "c")
    in_specs = (P(outer + inner, None), P(), P(inner, None), P(inner, None), P(outer + inner, None))
    out_specs = (P(outer + inner, None), P(outer + inner, None), P(inner, outer))
    return jax.shard_map(
        on_device, mesh=fine, in_specs=in_specs, out_specs=out_specs, check_vma=False
    )
```

```python
import functools

import jax
import jax.numpy as jnp
import numpy as np
from jax import lax
from jax.experimental import pallas as pl
from jax.experimental.pallas import tpu as pltpu
from jax.sharding import Mesh, PartitionSpec as P

BF, F32 = jnp.bfloat16, jnp.float32
NZ, NYL, NYH, NX, NC = 8, 2, 2, 4, 2
AXES = ("z", "yl", "yh", "x", "c")
SIZES = (NZ, NYL, NYH, NX, NC)
BLK, HALF = 512, 256
COLS = (((1,), (1,)), ((), ()))


def permute(array, target):
    pairs = []
    for flat_id in range(256):
        z, yl, yh, x, c = np.unravel_index(flat_id, SIZES)
        to = target(z, yh * 2 + yl, x, c)
        if to is not None:
            z, y, x, c = to[0] % NZ, to[1] % 4, to[2] % NX, to[3] % NC
            pairs.append((flat_id, int(np.ravel_multi_index((z, y % 2, y // 2, x, c), SIZES))))
    return lax.ppermute(array, AXES, pairs)


def swap_core(array):
    return permute(array, lambda z, y, x, c: (z, y, x, c + 1))


def first_axis(array, step):
    return permute(
        array, lambda z, y, x, c: (z, y, x + step, c) if c == 0 else (z, y + step, x, c)
    )


def second_axis(array, step):
    return permute(
        array, lambda z, y, x, c: (z, y + step, x, c) if c == 0 else (z, y, x + step, c)
    )


ORIGIN = (
    ((0, 0), (1, 0), (2, 0), (3, 0), (0, 1), (1, 1), (2, 1), (3, 1)),
    ((0, 0), (0, 1), (1, 0), (3, 1), (1, 1), (2, 0), (3, 0), (2, 1)),
)


def block_of(where, core, entry):
    hops = [ORIGIN[core_id][entry] for core_id in range(2)]
    hop = jnp.where(core == 0, hops[0][0], hops[1][0])
    flip = jnp.where(core == 0, hops[0][1], hops[1][1])
    return (where[2] + flip) % NYH * NX + (where[0] + NX - hop) % NX


def gather_first(array, step):
    def target(z, y, x, c):
        if c == 0:
            return z, y, x + step, c
        return ((z, y + 2, x, c), (z, y, x + 1, c), (z, y + 2, x - 1, c))[step - 1]

    return permute(array, target)


def gather_second(array, step):
    def target(z, y, x, c):
        return (z, y + 2, x, c) if c == 0 else (z, y, x + step, c)

    return permute(array, target)


def along_z(array, step):
    return permute(array, lambda z, y, x, c: (z + step, y, x, c))


COSTLY = ("sum", "finish")
MARK = jax.ShapeDtypeStruct((8, 128), F32)


def vmem():
    return pl.BlockSpec(memory_space=pltpu.VMEM)


def smem():
    return pl.BlockSpec(memory_space=pltpu.SMEM)


def anywhere():
    return pl.BlockSpec(memory_space=pl.ANY)


def call(kernel, name, outs, grid_args, limit, flops, size, **kw):
    return pl.pallas_call(
        kernel,
        name=name,
        out_shape=outs,
        compiler_params=pltpu.CompilerParams(vmem_limit_bytes=limit * 2**20),
        cost_estimate=pl.CostEstimate(
            flops=flops if name in COSTLY else 1, bytes_accessed=size if name in COSTLY else 1, transcendentals=0
        ),
        **grid_args,
        **kw,
    )


def arr(shape, dtype=BF):
    return jax.ShapeDtypeStruct(shape, dtype)


def flat(inputs, outputs, unused=0):
    return dict(
        in_specs=[smem()] + [vmem()] * inputs + [anywhere()] * unused,
        out_specs=[vmem()] * outputs,
    )


def rows_spec(cols):
    return pl.BlockSpec((64, cols), lambda r: (r, 0))


def prep_kernel(
    where, tokens, key_grad, codes, scales, gain, send, keep, scaled, inverse, weight, other, row
):
    @pl.when(pl.program_id(0) == 0)
    def _():
        row[...] = jnp.broadcast_to(gain[...], (8, BLK))
        column = jnp.broadcast_to(gain[...], (8, BLK)).T[:, :1]
        for group in range(4):
            rows = slice(group * 128, group * 128 + 128)
            to = slice((group % 2) * 128, (group % 2) * 128 + 128)
            part = codes[rows, :].astype(F32) * scales[group : group + 1, :]
            part = (part * column[rows]).astype(BF)

            @pl.when(where[4] % 2 == group // 2)
            def _():
                weight[to, :] = part

            @pl.when(where[4] % 2 != group // 2)
            def _():
                other[to, :] = part

    c = where[3]
    squares = jnp.zeros((64, 128), F32)
    for block in range(16):
        values = tokens[:, block * BLK : (block + 1) * BLK].astype(F32)
        values = values * values
        for lane in range(4):
            squares += values[:, lane * 128 : (lane + 1) * 128]
    for block in range(8):
        col = pl.multiple_of((block * NC + 1 - c) * BLK, BLK)
        send[:, block * BLK : (block + 1) * BLK] = tokens[:, pl.ds(col, BLK)]
        col = pl.multiple_of((block * NC + c) * BLK, BLK)
        keep[:, block * BLK : (block + 1) * BLK] = tokens[:, pl.ds(col, BLK)]
    inv = lax.rsqrt(jnp.sum(squares, axis=-1, keepdims=True) / 8192.0 + 1e-05)
    inverse[...] = jnp.broadcast_to(inv, (64, 128))
    kg = (key_grad[...].astype(F32) * inv).astype(BF)
    scaled[...] = kg
    send[:, 4096:] = kg


def partial_kernel(steps, where, tok_own, tok_far, kg_own, *refs):
    *outs, mark, kgt = refs
    mark[...] = jnp.zeros_like(mark)
    x, c = where[0], where[3]
    y = where[2] * 2 + where[1]
    for side, kg in enumerate((kg_own[...], tok_far[:, 4096:])):
        turned = kg.T
        for row in range(16):
            to = (row % 2) * 256 + (row // 2) * 32
            kgt[to : to + 32, side * 256 : side * 256 + 256] = turned[row * 32 : row * 32 + 32, :]
    for step, out in zip(steps, outs):
        to_x, to_y = (x + step) % NX, (y + step) % 4
        for rh in range(2):
            for ch in range(2):
                row = jnp.where(c == 0, rh, to_y % 2)
                block = jnp.where(c == 0, ch * NX + to_x, (to_y // 2) * NX + rh * 2 + ch)
                left = kgt[pl.ds(pl.multiple_of(row * 256, 256), 256), :]
                cols = pl.ds(pl.multiple_of(block * BLK, BLK), BLK)
                value = jnp.dot(
                    left[:, :256], tok_own[:, cols], preferred_element_type=F32
                ) + jnp.dot(left[:, 256:], tok_far[:, cols], preferred_element_type=F32)
                out[rh * 256 : rh * 256 + 256, ch * BLK : ch * BLK + BLK] = value.astype(BF)


def add(parts, rows, cols):
    out = parts[0][rows, cols].astype(F32)
    for part in parts[1:]:
        out = out + part[rows, cols].astype(F32)
    return out.astype(BF)


def cut_kernel(where, *refs):
    parts, outs, mark = refs[:4], refs[-5:-1], refs[-1]
    mark[...] = jnp.zeros_like(mark)
    c = where[3]
    for step in range(4):
        to_x, to_y = (where[0] + step) % NX, (where[2] * 2 + where[1] + step) % 4
        row = jnp.where(c == 0, to_y % 2, to_x // 2)
        col = jnp.where(c == 0, to_y // 2, to_x % 2)
        outs[step][...] = add(
            parts, pl.ds(pl.multiple_of(row * 256, 256), 256), pl.ds(pl.multiple_of(col * BLK, BLK), BLK)
        )


def sum_kernel(where, gain, *refs):
    total = refs[0][...].astype(F32)
    for part in refs[1:4]:
        total = total + part[...].astype(F32)
    refs[5][...] = (total * gain[:1, :]).astype(BF)


def end_kernel(where, parts, after, out):
    out[...] = jnp.sum(parts[...].astype(F32), axis=0)


def pick_kernel(where, weight, near_1, near_2, near_3, after, rows, send_1, send_2):
    rows[:HALF, :] = near_1[...]
    rows[HALF:BLK, :] = near_2[...]
    rows[BLK:, :] = near_3[...]
    send_2[HALF:, :] = near_3[...]

    @pl.when(where[3] == 0)
    def _():
        send_1[:HALF, :] = weight[...]
        send_1[HALF:, :] = near_1[...]
        send_2[:HALF, :] = near_2[...]

    @pl.when(where[3] != 0)
    def _():
        send_1[:HALF, :] = near_1[...]
        send_1[HALF:, :] = near_2[...]
        send_2[:HALF, :] = weight[...]


def relay_kernel(where, source, after, out_1, out_2):
    out_1[...] = source[:HALF, :]
    out_2[...] = source[HALF:, :]


def project_kernel(first, where, tok_own, tok_far, kg_own, *refs):
    key_own, key_far, grad_own, grad_far, mark = refs[-5:]
    mark[...] = jnp.zeros_like(mark)
    if first == 0:
        key_own[...] = jnp.zeros_like(key_own)
        key_far[...] = jnp.zeros_like(key_far)
    else:
        key_own[...] = refs[5][...]
        key_far[...] = refs[6][...]
    pieces = [ref.at[row : row + HALF, :] for ref in refs[: 5 if first else 4] for row in range(0, ref.shape[0], HALF)]
    if first == 0:
        pieces = [pieces[index] for index in (0, 2, 3, 4, 1, 5, 6, 7)]
    for index, piece in enumerate(pieces):
        half = (where[4] + index // 4) % 2
        block = block_of(where, where[3], first + index % 4)
        cols = pl.ds(pl.multiple_of(block * BLK + half * HALF, HALF), HALF)
        to = slice(index * HALF, (index + 1) * HALF)
        weight = piece[...]
        key_own[...] += jnp.dot(tok_own[:, cols], weight, preferred_element_type=F32)
        key_far[...] += jnp.dot(tok_far[:, cols], weight, preferred_element_type=F32)
        for kg, grad in ((kg_own[...], grad_own), (tok_far[:, 4096:], grad_far)):
            grad[:, to] = lax.dot_general(kg, weight, COLS, preferred_element_type=F32).astype(BF)


def finish_kernel(where, tokens, *refs):
    grads, (key_a, key_b, kg, inverse, key_out, token_grad, mark) = refs[:4], refs[4:]
    mark[...] = jnp.zeros_like(mark)
    c, z = where[3], where[4]
    inv = inverse[:, :1]
    key_sum = key_a[...] + key_b[...]
    key_out[...] = (key_sum * inv).astype(BF)
    dotted = jnp.sum(kg[...].astype(F32) * key_sum, axis=-1, keepdims=True) / 8192.0
    slope = inv * inv * inv * dotted
    for source, grad in enumerate(grads):
        core = (c + source // 2) % 2
        for index in range(8):
            half = (z + index // 4) % 2
            block = block_of(where, core, (source % 2) * 4 + index % 4)
            cols = pl.ds(pl.multiple_of((block * NC + core) * BLK + half * HALF, HALF), HALF)
            part = grad[:, index * HALF : (index + 1) * HALF].astype(F32)
            token_grad[:, cols] = (part - tokens[:, cols].astype(F32) * slope).astype(BF)


def on_device(tokens, norm_gain, weight_codes, weight_scales, key_grad):
    x, yl, yh, c, z = [lax.axis_index(name) for name in ("x", "yl", "yh", "c", "z")]
    shard = (yh * NX + x) * NC + c
    where = jnp.stack([x, yl, yh, c, z, shard]).astype(jnp.int32)
    tokens, key_grad, weight_codes, weight_scales, gains = [
        pltpu.with_memory_space_constraint(array, pltpu.HBM)
        for array in (tokens, key_grad, weight_codes, weight_scales, norm_gain.reshape(1, 8192))
    ]

    def fixed(rows, cols):
        return pl.BlockSpec((rows, cols), lambda r, w: (0, 0))

    def moving(cols):
        return pl.BlockSpec((64, cols), lambda r, w: (r, 0))

    send, keep, kg, inverse, weight, weight_other, gain_row = call(
        prep_kernel,
        "prep",
        [arr((256, 4608)), arr((256, 4096)), arr((256, 512)), arr((256, 128), F32)]
        + [arr((HALF, 512))] * 2
        + [arr((8, BLK), F32)],
        dict(
            grid_spec=pltpu.PrefetchScalarGridSpec(
                num_scalar_prefetch=1,
                grid=(4,),
                in_specs=[
                    moving(8192),
                    moving(512),
                    fixed(BLK, 512),
                    fixed(4, 512),
                    pl.BlockSpec((1, BLK), lambda r, w: (0, w[5])),
                ],
                out_specs=[moving(4608), moving(4096), moving(512), moving(128)]
                + [fixed(HALF, 512)] * 2
                + [fixed(8, BLK)],
            )
        ),
        14,
        2**22,
        9 * 2**20,
    )(where, tokens, key_grad, weight_codes, weight_scales, gains)
    near = [gather_first(weight, s) for s in (1, 2, 3)]
    tok_far = swap_core(send)

    *parts, partial_mark = call(
        functools.partial(partial_kernel, range(4)),
        "partial",
        [arr((512, 1024))] * 4 + [MARK],
        flat(3, 5),
        16,
        2**31,
        9 * 2**20,
        scratch_shapes=[pltpu.VMEM((512, 512), BF)],
    )(where, keep, tok_far, kg)

    near_rows, send_1, send_2 = call(
        pick_kernel,
        "pick",
        [arr((768, 512)), arr((512, 512)), arr((512, 512))],
        flat(4, 3, 1),
        8,
        2**18,
        3 * 2**20,
    )(where, weight, *near, partial_mark)
    got_1, got_2 = gather_second(send_1, 1), gather_second(send_2, 3)


    def project(first, *operands, unused=0):
        return call(
            functools.partial(project_kernel, first),
            "project",
            [arr((256, 512), F32)] * 2 + [arr((256, 2048))] * 2 + [MARK],
            flat(len(operands) - unused, 5, unused),
            16,
            2**31,
            10 * 2**20,
        )(where, *operands)

    key_1, key_far_1, grad_1, grad_far_1, early_mark = project(
        0, keep, tok_far, kg, weight, weight_other, near_rows, along_z(near_rows, 1)
    )
    relayed_1, relayed_2 = call(
        relay_kernel,
        "relay",
        [arr((HALF, 512))] * 2,
        flat(1, 2, 1),
        8,
        2**18,
        2**20,
    )(where, got_2, early_mark)
    *cuts, cut_mark = call(cut_kernel, "cut", [arr((256, 512))] * 4 + [MARK], flat(4, 5, 1), 10, 2**20, 5 * 2**20)(
        where,
        parts[0],
        first_axis(parts[1], 1),
        first_axis(parts[2], 2),
        first_axis(parts[3], 3),
        early_mark,
    )
    crossed = [second_axis(cuts[s], s) for s in (1, 2, 3)]
    key_2, key_far_2, grad_2, grad_far_2, project_mark = project(
        4,
        keep,
        tok_far,
        kg,
        got_1,
        got_2,
        along_z(got_1, 1),
        along_z(relayed_1, 1),
        along_z(relayed_2, -1),
        key_1,
        key_far_1,
        cut_mark,
        unused=1,
    )

    plane = call(
        sum_kernel,
        "sum",
        arr((256, 512)),
        dict(in_specs=[smem()] + [vmem()] * 5 + [anywhere()], out_specs=vmem()),
        8,
        14 * 10**9,
        5 * 2**18,
    )(where, gain_row, cuts[0], *crossed, project_mark)
    over_z = lax.all_to_all(
        plane.reshape(NZ, 32, BLK), "z", split_axis=0, concat_axis=0, tiled=True
    )
    key_out, token_grad, finish_mark = call(
        finish_kernel,
        "finish",
        [arr((256, 512)), arr((256, 8192)), MARK],
        dict(
            grid=(4,),
            in_specs=[smem(), rows_spec(8192)]
            + [rows_spec(2048)] * 4
            + [rows_spec(n) for n in (512, 512, 512, 128)],
            out_specs=[rows_spec(512), rows_spec(8192), pl.BlockSpec((8, 128), lambda r: (0, 0))],
        ),
        14,
        2**23,
        13 * 2**20,
    )(
        where,
        tokens,
        grad_1,
        grad_2,
        swap_core(grad_far_1),
        swap_core(grad_far_2),
        key_2,
        swap_core(key_far_2),
        key_grad,
        inverse,
    )
    weight_grad = call(
        end_kernel,
        "end",
        arr((32, BLK), F32),
        dict(in_specs=[smem(), vmem(), anywhere()], out_specs=vmem()),
        8,
        2**17,
        2**19,
    )(where, over_z, finish_mark).T
    return key_out, token_grad, weight_grad


def solution(mesh):
    fine = Mesh(np.asarray(mesh.devices).reshape(SIZES), AXES)
    outer, inner = ("z", "yl"), ("yh", "x", "c")
    in_specs = (P(outer + inner, None), P(), P(inner, None), P(inner, None), P(outer + inner, None))
    out_specs = (P(outer + inner, None), P(outer + inner, None), P(inner, outer))
    return jax.shard_map(
        on_device, mesh=fine, in_specs=in_specs, out_specs=out_specs, check_vma=False
    )
```
